512 devices in a mesh: dp: 32 (over z_hi, x, core), tensor: 16 (over y, z_lo).
Axes of the slice: x: 4, y: 4, z: 16 (z_hi: 4, z_lo: 4; z = z_hi * 4 + z_lo), core: 2. Of those that a mesh axis runs over, the one named last changes fastest.
Arguments:
- weight: bfloat16 [16384, 4096], P('tensor', 'dp'), may hold values from -0.046875 to 0.046875
- inputs: bfloat16 [16384, 16384], P('dp', 'tensor'), may hold values from -6 to 6
- cotangent: bfloat16 [16384, 4096], P('dp', 'tensor'), may hold values from -30 to 30
- projector: bfloat16 [16384, 1024], P('tensor'), may hold values from -0.046875 to 0.046875
- first_moment: float32 [1024, 4096], P('dp', 'tensor'), may hold values from -18 to 18
- second_moment: float32 [1024, 4096], P('dp', 'tensor'), may hold values from 0.2 to 2
Outputs:
- new_weight: bfloat16 [16384, 4096], P('tensor', 'dp')
- new_first: float32 [1024, 4096], P('dp', 'tensor')
- new_second: float32 [1024, 4096], P('dp', 'tensor')
The draws below stay inside these ranges and needn't reach their ends.
All inputs are finite; a program needn't handle non-finite values.
Results may differ from the reference program's by a relative error of at most 0.0053.
Values may be sent and summed in bfloat16 or wider, within the bound.
A program may use at most 64 MiB of HBM per device.

```python
import math
import jax
import jax.numpy as jnp
from jax import lax

M = 16384
R = 1024
N = 4096
TOK = 512
STEP = 10
REPLICAS = 32
TOKENS = 16384


def raised(array, key, source, target, shards_of, factor):
    def block_of(position):
        return (jnp.arange(array.shape[position]) // (array.shape[position] // shards_of)).reshape((-1,) + (1,) * (array.ndim - 1 - position))

    one_side = jax.random.permutation(key, shards_of)[block_of(target)]
    other_side = (block_of(target) + shards_of // 2) % shards_of
    return jnp.where((block_of(source) == one_side) | (block_of(source) == other_side), factor * array, array)


def level_of(key, shape, shards, low, high):
    factor_of, own = 1.0, jax.random.fold_in(key, 6)
    for axis_at, parts in shards:
        heights = jnp.exp(jax.random.uniform(jax.random.fold_in(own, axis_at), (parts,), jnp.float32, low / len(shards), high / len(shards)))
        factor_of = factor_of * jnp.repeat(heights, shape[axis_at] // parts).reshape([-1 if axis == axis_at else 1 for axis in range(len(shape))])
    return factor_of


def scatter_about(stream_key, shape, width, most, cuts=(), kind=jnp.bfloat16):
    drawn = width * jax.random.normal(stream_key, shape, jnp.float32)
    if cuts:
        drawn = drawn * level_of(stream_key, shape, cuts, -0.22, 0.18)
    return jnp.clip(drawn, -most, most).astype(kind)


def bell_draw_with(stream_key, extent, deviation, bound, split, heavy, kind=jnp.bfloat16):
    values = deviation * jax.random.normal(stream_key, extent, jnp.float32)
    if split:
        values = values * level_of(stream_key, extent, split, -0.22, 0.18)
    return jnp.clip(raised(values, jax.random.fold_in(stream_key, 3), *heavy), -bound, bound).astype(kind)


def setup_inputs(seed: int = 0) -> dict:
    key_list = jax.random.split(jax.random.key(seed), 7)
    weight = scatter_about(key_list[0], (M, N), M ** -0.5, 0.046875, ((0, 16), (1, 32)))
    inputs = scatter_about(key_list[1], (TOKENS, M), 1.0, 6.0, ((0, 32), (1, 16)))
    cotangent = bell_draw_with(key_list[2], (TOKENS, N), (20.0 * (REPLICAS / TOK) ** 0.5), 30.0, ((0, 32), (1, 16)), (0, 1, 32, 2.75))
    projector = scatter_about(key_list[3], (M, R), M ** -0.5, 0.046875, ((0, 16),))
    first_moment = scatter_about(key_list[4], (R, N), 3.0, 18.0, ((0, 32), (1, 16)), jnp.float32)
    second_moment = jnp.clip(jnp.exp(math.log(2.0) - 2.3025851 * jax.random.uniform(key_list[5], (R, N), jnp.float32) ** level_of(key_list[5], (R, N), ((0, 32), (1, 16)), -0.2, 0.2)), 0.2, 2.0)
    return dict(weight=weight, inputs=inputs, cotangent=cotangent, projector=projector, first_moment=first_moment, second_moment=second_moment)


def reference(weight, inputs, cotangent, projector, first_moment, second_moment):
    projected = jnp.dot(inputs, projector, preferred_element_type=jnp.float32).astype(jnp.bfloat16)
    low = lax.dot_general(projected, cotangent, (((0,), (0,)), ((), ())), preferred_element_type=jnp.float32) / REPLICAS
    new_first = 0.9 * first_moment + 0.1 * low
    new_second = 0.999 * second_moment + 0.001 * low * low
    first_hat = new_first / (1.0 - 0.9 ** STEP)
    second_hat = new_second / (1.0 - 0.999 ** STEP)
    update = (first_hat / (jnp.sqrt(second_hat) + 1e-08)).astype(jnp.bfloat16)
    change = jnp.dot(projector, update, preferred_element_type=jnp.float32)
    new_weight = (weight.astype(jnp.float32) - 0.5 * change).astype(jnp.bfloat16)
    return (new_weight, new_first, new_second)
```

```python
import jax
import jax.numpy as jnp
from jax import lax
from jax.experimental import pallas as pl
from jax.experimental.pallas import tpu as pltpu
from jax.sharding import PartitionSpec as P

STEP = 10
REPLICAS = 32
MESH = pl.DeviceIdType.MESH
F32, BF16 = jnp.float32, jnp.bfloat16


def kernel(
    w_hbm, x_hbm, ct_hbm, p_hbm, m1_hbm, m2_hbm,
    ow, o1, o2,
    w_v, x_v, ct_v, p_v, m1_v, m2_v,
    part, y1s, y1r, y2s, y2r, ysum, zs, zr, proj,
    plow, cs, cr, csum, xs, xr, xsum, hs, hr, upd, need, acc,
    lsem, ssem, rsem,
):
    dp, t = lax.axis_index("dp"), lax.axis_index("tensor")
    zh, x, c = lax.div(dp, 8), lax.rem(lax.div(dp, 2), 4), lax.rem(dp, 2)
    y, zl = lax.div(t, 4), lax.rem(t, 4)
    xh, xx = lax.div(x, 2), lax.rem(x, 2)
    zlh = lax.div(zl, 2)
    plus = lambda v, k: lax.rem(v + k, 4)
    yp, y2, ym = plus(y, 1), plus(y, 2), plus(y, 3)
    other = 1 - c

    def dev(zh_=zh, x_=x, c_=c, y_=y, zl_=zl):
        return {"dp": zh_ * 8 + x_ * 2 + c_, "tensor": y_ * 4 + zl_}

    y_up, y_down = dev(y_=yp), dev(y_=ym)
    moved = (zh != y) | (x != zl)
    across = [dev(y, zl, c, zh, x), dev(y, zl, other, zh, x)]

    count = {"l": 0, "r": 0}

    def load(src, dst):
        copy = pltpu.make_async_copy(src, dst, lsem.at[count["l"]])
        count["l"] += 1
        copy.start()
        return copy

    barrier = pltpu.get_barrier_semaphore()
    partners = [y_up, y_down, dev(c_=other)]
    partners += [dev(zl_=plus(zl, k)) for k in (1, 2, 3)]
    partners += [dev(x_=plus(x, k)) for k in (1, 2, 3)]
    partners += [dev(zh_=plus(zh, k)) for k in (1, 2, 3)]

    def signal(device):
        pl.semaphore_signal(barrier, inc=1, device_id=device, device_id_type=MESH)

    for device in partners:
        signal(device)

    @pl.when(moved)
    def _():
        signal(across[0])
        signal(across[1])

    x_load = [load(x_hbm.at[pl.ds(y2 * 128, 128)], x_v.at[y2])]
    p_load = []
    for s in range(4):
        h, q = divmod(s, 2)
        pair = []
        for i in range(2):
            col = (2 * q + i) * 256 + h * 128
            pair.append(load(p_hbm.at[:, pl.ds(col, 128)], p_v.at[s, :, pl.ds(i * 128, 128)]))
        p_load.append(pair)
        if s == 0:
            for b in (yp, ym, y):
                x_load.append(load(x_hbm.at[pl.ds(b * 128, 128)], x_v.at[b]))
    ct_load = load(ct_hbm, ct_v)
    m_load = [load(m1_hbm, m1_v), load(m2_hbm, m2_v)]
    w_load = load(w_hbm, w_v)

    sends = []

    def copy_of(src, dst, device, index):
        return pltpu.make_async_remote_copy(
            src_ref=src, dst_ref=dst, send_sem=ssem.at[index], recv_sem=rsem.at[index],
            device_id=device, device_id_type=MESH,
        )

    def new():
        count["r"] += 1
        return count["r"] - 1

    def send(src, dst, device, index):
        copy = copy_of(src, dst, device, index)
        copy.start()
        sends.append(copy)

    def arrived(dst, index):
        copy_of(dst, dst, y_up, index).wait_recv()

    ids = {}

    def sem(*key):
        if key not in ids:
            ids[key] = new()
        return ids[key]

    def dot(a, b):
        return jnp.dot(a, b, preferred_element_type=F32)

    def rows(b, n=4):
        return pl.ds(b * 4, n)

    def project(s, b):
        part[s, rows(b)] = dot(x_v[b], p_v[s]).reshape(4, 32, 256)

    def a0(s):
        for copy in p_load[s]:
            copy.wait()
        if s == 0:
            x_load[0].wait()
        project(s, y2)
        y1s[s] = part[s, rows(y2)].astype(BF16)
        if s == 0:

            @pl.when(moved)
            def _():
                pl.semaphore_wait(barrier, 14)

            @pl.when(jnp.logical_not(moved))
            def _():
                pl.semaphore_wait(barrier, 12)

        send(y1s.at[s, pl.ds(0, 2)], y1r.at[s, 0], y_up, sem("y1u", s))
        send(y1s.at[s, pl.ds(2, 2)], y1r.at[s, 1], y_down, sem("y1d", s))
        if s == 0:
            for copy in x_load[1:]:
                copy.wait()


        project(s, yp)
        project(s, ym)
        project(s, y)

    def a1(s):
        up, down = part[s, rows(yp)], part[s, rows(ym)]
        arrived(y1r.at[s, 0], sem("y1u", s))
        y2s[s, 0, 0:2] = (up[0:2] + y1r[s, 0].astype(F32)).astype(BF16)
        y2s[s, 0, 2:4] = up[2:4].astype(BF16)
        send(y2s.at[s, 0], y2r.at[s, 0], y_up, sem("y2u", s))
        arrived(y1r.at[s, 1], sem("y1d", s))
        y2s[s, 1, 0:2] = down[0:2].astype(BF16)
        y2s[s, 1, 2:4] = (down[2:4] + y1r[s, 1].astype(F32)).astype(BF16)
        send(y2s.at[s, 1], y2r.at[s, 1], y_down, sem("y2d", s))

    def a2(s):
        arrived(y2r.at[s, 0], sem("y2u", s))
        arrived(y2r.at[s, 1], sem("y2d", s))
        total = part[s, rows(y)] + y2r[s, 0].astype(F32) + y2r[s, 1].astype(F32)
        ysum[s] = total
        zs[s] = total.astype(BF16)
        for k in (2, 1, 3):
            to = plus(zl, k)
            send(zs.at[s, to], zr.at[s, k - 1], dev(zl_=to), sem("z", s, k))

    def a3(s):
        total = ysum[s, zl]
        for k in (1, 2, 3):
            arrived(zr.at[s, k - 1], sem("z", s, k))
            total = total + zr[s, k - 1].astype(F32)
        proj[s, t] = total.astype(BF16)
        for k in (2, 1, 3):
            send(proj.at[s, t], proj.at[s, t], dev(zl_=plus(zl, k)), sem("za", s, k))

    def a4(s):
        for k in (1, 2, 3):
            arrived(proj.at[s, y * 4 + plus(zl, 4 - k)], sem("za", s, k))
        mine = proj.at[s, rows(y)]
        send(mine, mine, y_up, sem("ya1u", s))
        send(mine, mine, y_down, sem("ya1d", s))

    def a5(s):
        arrived(proj.at[s, rows(ym)], sem("ya1u", s))
        first = proj.at[s, rows(ym, 2)]
        send(first, first, y_up, sem("ya2u", s))
        arrived(proj.at[s, rows(yp)], sem("ya1d", s))
        second = proj.at[s, pl.ds(yp * 4 + 2, 2)]
        send(second, second, y_down, sem("ya2d", s))

    def a6(s):
        h, q = divmod(s, 2)
        arrived(proj.at[s, rows(y2, 2)], sem("ya2u", s))
        arrived(proj.at[s, pl.ds(y2 * 4 + 2, 2)], sem("ya2d", s))
        if s == 0:
            ct_load.wait()
        block = lax.dot_general(
            proj[s].reshape(512, 256), ct_v[...], (((0,), (0,)), ((), ())), preferred_element_type=F32
        ).reshape(2, 2, 2, 32, 256)
        for zz in range(2):
            for i in range(2):
                for cc in range(2):
                    plow[h, cc, i, 2 * q + zz] = block[zz, i, cc]
        if q == 1:
            cs[h] = plow[h, other].astype(BF16)
            send(cs.at[h], cr.at[h], dev(c_=other), sem("c", h))

    def b0(h):
        arrived(cr.at[h], sem("c", h))
        total = plow[h, c] + cr[h].astype(F32)
        csum[h] = total
        xs[h] = total.astype(BF16)
        for k in (2, 1, 3):
            to = plus(x, k)
            index = sem("x", k)

            @pl.when(lax.div(to, 2) == h)
            def _():
                copy_of(xs.at[h, lax.rem(to, 2)], xr.at[k - 1], dev(x_=to), index).start()

    def b1(h):
        for k in (1, 2, 3):
            sem("h", k)

        @pl.when(xh == h)
        def _():
            total = csum[h, xx]
            for k in (1, 2, 3):
                arrived(xr.at[k - 1], sem("x", k))
                total = total + xr[k - 1].astype(F32)
            xsum[...] = total
            hs[...] = total.astype(BF16)
            for k in (2, 1, 3):
                to = plus(zh, k)
                copy_of(hs.at[to], hr.at[k - 1], dev(zh_=to), sem("h", k)).start()

    def b2(h):
        for k in (0, 1):
            sem("t", k)
        if h == 0:
            for copy in m_load:
                copy.wait()

        @pl.when(xh == h)
        def _():
            total = xsum[zh]
            for k in (1, 2, 3):
                arrived(hr.at[k - 1], sem("h", k))
                total = total + hr[k - 1].astype(F32)
            low = total / REPLICAS
            first = 0.9 * m1_v[...] + 0.1 * low
            second = 0.999 * m2_v[...] + 0.001 * low * low
            o1[...] = first
            o2[...] = second
            first_hat = first / (1.0 - 0.9**STEP)
            second_hat = second / (1.0 - 0.999**STEP)
            update = (first_hat / (jnp.sqrt(second_hat) + 1e-08)).astype(BF16)
            upd[0] = update[:, :128]
            upd[1] = update[:, 128:]

            @pl.when(moved)
            def _():
                copy_of(upd.at[c], need.at[dp], across[0], sem("t", 0)).start()

            @pl.when(jnp.logical_not(moved))
            def _():
                pltpu.make_async_copy(upd.at[c], need.at[dp], rsem.at[sem("t", 0)]).start()

            copy_of(upd.at[other], need.at[dp], across[1], sem("t", 1)).start()

    def c0(h):
        for k in (1, 2, 3):
            sem("n", k)

        @pl.when(zlh == h)
        def _():
            arrived(need.at[t * 2 + c], sem("t", 0))
            arrived(need.at[t * 2 + other], sem("t", 1))
            mine = need.at[pl.ds(t * 2, 2)]
            for k in (2, 1, 3):
                copy_of(mine, mine, dev(zl_=plus(zl, k)), sem("n", k)).start()

    def c1(h):
        for k in (1, 2, 3):
            source = plus(zl, 4 - k)

            @pl.when(lax.div(source, 2) == h)
            def _():
                arrived(need.at[pl.ds((y * 4 + source) * 2, 2)], sem("n", k))

        mine = need.at[pl.ds(y * 8 + h * 4, 4)]
        send(mine, mine, y_up, sem("n1u", h))
        send(mine, mine, y_down, sem("n1d", h))

    def c2(h):
        arrived(need.at[pl.ds(ym * 8 + h * 4, 4)], sem("n1u", h))
        first = need.at[pl.ds(ym * 8 + h * 4, 2)]
        send(first, first, y_up, sem("n2u", h))
        arrived(need.at[pl.ds(yp * 8 + h * 4, 4)], sem("n1d", h))
        second = need.at[pl.ds(yp * 8 + h * 4 + 2, 2)]
        send(second, second, y_down, sem("n2d", h))

    def d(h):
        arrived(need.at[pl.ds(y2 * 8 + h * 4, 2)], sem("n2u", h))
        arrived(need.at[pl.ds(y2 * 8 + h * 4 + 2, 2)], sem("n2d", h))
        lower = [need[zz * 8 + h * 4 : zz * 8 + h * 4 + 4].reshape(128, 128) for zz in range(4)]
        left = jnp.concatenate(lower[:2], axis=0)
        right = jnp.concatenate(lower[2:], axis=0)
        for r in range(0, 1024, 256):
            span = slice(r, r + 256)
            change = dot(p_v[2 * h, span], left) + dot(p_v[2 * h + 1, span], right)
            if h == 0:
                acc[span] = change
            else:
                ow[span] = (w_v[span].astype(F32) - 0.5 * (acc[span] + change)).astype(BF16)

    plan = []
    for s in range(4):
        for j, stage in enumerate((a0, a1, a2, a3, a4, a5, a6)):
            plan.append((s + j, 0, -j, stage, s))
    for h in range(2):
        for j, stage in enumerate((b0, b1, b2, c0, c1, c2, d)):
            plan.append((8 + 2 * h + j, 1, -j, stage, h))
    for tick, _, _, stage, index in sorted(plan, key=lambda e: e[:3]):
        stage(index)
        if stage is b2 and index == 1:
            w_load.wait()

    for copy in sends:
        copy.wait_send()
    for k in (1, 2, 3):
        copy_of(xs.at[0, 0], xr.at[k - 1], y_up, sem("x", k)).wait_send()
        copy_of(hs.at[0], hr.at[k - 1], y_up, sem("h", k)).wait_send()
        copy_of(need.at[pl.ds(0, 2)], need.at[pl.ds(0, 2)], y_up, sem("n", k)).wait_send()

    @pl.when(moved)
    def _():
        copy_of(upd.at[0], need.at[0], y_up, sem("t", 0)).wait_send()

    copy_of(upd.at[0], need.at[0], y_up, sem("t", 1)).wait_send()


def local(weight, inputs, cotangent, projector, first_moment, second_moment):
    v = pltpu.VMEM
    return pl.pallas_call(
        kernel,
        out_shape=(
            jax.ShapeDtypeStruct((1024, 128), BF16),
            jax.ShapeDtypeStruct((32, 256), F32),
            jax.ShapeDtypeStruct((32, 256), F32),
        ),
        in_specs=[pl.BlockSpec(memory_space=pl.ANY)] * 6,
        out_specs=[pl.BlockSpec(memory_space=pltpu.VMEM)] * 3,
        scratch_shapes=[
            v((1024, 128), BF16),
            v((4, 128, 1024), BF16),
            v((512, 256), BF16),
            v((4, 1024, 256), BF16),
            v((32, 256), F32),
            v((32, 256), F32),
            v((4, 16, 32, 256), F32),
            v((4, 4, 32, 256), BF16),
            v((4, 2, 2, 32, 256), BF16),
            v((4, 2, 4, 32, 256), BF16),
            v((4, 2, 4, 32, 256), BF16),
            v((4, 4, 32, 256), F32),
            v((4, 4, 32, 256), BF16),
            v((4, 3, 32, 256), BF16),
            v((4, 16, 32, 256), BF16),
            v((2, 2, 2, 4, 32, 256), F32),
            v((2, 2, 4, 32, 256), BF16),
            v((2, 2, 4, 32, 256), BF16),
            v((2, 2, 4, 32, 256), F32),
            v((2, 2, 4, 32, 256), BF16),
            v((3, 4, 32, 256), BF16),
            v((4, 32, 256), F32),
            v((4, 32, 256), BF16),
            v((3, 32, 256), BF16),
            v((2, 32, 128), BF16),
            v((32, 32, 128), BF16),
            v((1024, 128), F32),
            pltpu.SemaphoreType.DMA((20,)),
            pltpu.SemaphoreType.DMA((96,)),
            pltpu.SemaphoreType.DMA((96,)),
        ],
        compiler_params=pltpu.CompilerParams(
            collective_id=0, has_side_effects=True, vmem_limit_bytes=40 * 2**20
        ),
    )(weight, inputs, cotangent, projector, first_moment, second_moment)


def solution(mesh):
    placed = (
        P("tensor", "dp"),
        P("dp", "tensor"),
        P("dp", "tensor"),
        P("tensor", None),
        P("dp", "tensor"),
        P("dp", "tensor"),
    )
    return jax.shard_map(
        local,
        mesh=mesh,
        in_specs=placed,
        out_specs=(P("tensor", "dp"), P("dp", "tensor"), P("dp", "tensor")),
        check_vma=False,
    )
```

```python
import jax
import jax.numpy as jnp
from jax import lax
from jax.experimental import pallas as pl
from jax.experimental.pallas import tpu as pltpu
from jax.sharding import PartitionSpec as P

STEP = 10
REPLICAS = 32
MESH = pl.DeviceIdType.MESH
F32, BF16 = jnp.float32, jnp.bfloat16


def kernel(
    w_hbm, x_hbm, ct_hbm, p_hbm, m1_hbm, m2_hbm,
    ow, o1, o2,
    w_v, x_v, ct_v, p_v, m_v, mr_v,
    ys, yr, yown, zs, zr, proj,
    plow, cs, cr, csum, xs, xr, xsum, hs, hr, low_v, back, upd, need, acc,
    lsem, ssem, rsem,
):
    dp, t = lax.axis_index("dp"), lax.axis_index("tensor")
    zh, x, c = lax.div(dp, 8), lax.rem(lax.div(dp, 2), 4), lax.rem(dp, 2)
    y, zl = lax.div(t, 4), lax.rem(t, 4)
    xh, xx = lax.div(x, 2), lax.rem(x, 2)
    other = 1 - c
    moved = zh != y
    apart = x != zl

    def plus(v, k):
        return lax.rem(v + k, 4)

    def dev(zh_=zh, x_=x, c_=c, y_=y, zl_=zl):
        return {"dp": zh_ * 8 + x_ * 2 + c_, "tensor": y_ * 4 + zl_}

    count = {"l": 0}
    ids = {}
    waits = []
    state = {"mute": False}

    def sem(*key):
        return ids.setdefault(key, len(ids))

    def load(src, dst):
        copy = pltpu.make_async_copy(src, dst, lsem.at[count["l"]])
        count["l"] += 1
        copy.start()
        return copy

    def copy_of(src, dst, device, index, at=None):
        return pltpu.make_async_remote_copy(
            src_ref=src, dst_ref=dst, send_sem=ssem.at[index],
            recv_sem=rsem.at[index if at is None else at], device_id=device, device_id_type=MESH,
        )

    def send(src, dst, device, index, at=None, like=None, cond=None):
        if not state["mute"]:
            copy_of(src, dst, device, index, at).start()
            waits.append((like or (lambda: src), index, cond))

    def arrived(dst, index):
        copy_of(dst, dst, dev(c_=other), index).wait_recv()

    def dot(a, b):
        return jnp.dot(a, b, preferred_element_type=F32)

    p_load, x_load = {}, []
    for k in (2, 1, 3, 0):
        b = plus(y, k)
        p_load[k] = load(p_hbm.at[:, pl.ds(pl.multiple_of(b * 256, 256), 256)], p_v.at[b])
        if k == 2:
            x_load.append(load(x_hbm, x_v))
    m_load = [load(m1_hbm, m_v.at[0]), load(m2_hbm, m_v.at[1])]
    ct_load = load(ct_hbm, ct_v.at[y])
    w_load = load(w_hbm, w_v)

    barrier = pltpu.get_barrier_semaphore()

    def signal(device):
        pl.semaphore_signal(barrier, inc=1, device_id=device, device_id_type=MESH)

    for k in (1, 2, 3):
        signal(dev(y_=plus(y, k)))
        signal(dev(zl_=plus(zl, k)))
        signal(dev(x_=plus(x, k)))
        signal(dev(zh_=plus(zh, k)))
    signal(dev(c_=other))
    for k in range(4):
        source = plus(x, k)
        signal(dev(x_=source, c_=other, zl_=x))
        if k == 0:

            @pl.when(apart)
            def _():
                signal(dev(zl_=x))
        else:
            signal(dev(x_=source, zl_=x))

    swapped = dev(zh_=y, y_=zh)

    @pl.when(moved)
    def _():
        signal(swapped)

    def enter():
        for far in (True, False):
            for off in (True, False):
                here = (moved if far else jnp.logical_not(moved)) & (apart if off else jnp.logical_not(apart))

                @pl.when(here)
                def _():
                    pl.semaphore_wait(barrier, 20 + far + off)

    def project(k):
        p_load[k].wait()
        return dot(x_v[...], p_v[plus(y, k)]).reshape(4, 2, 64, 256)

    def give_y(k, h, u):
        send(ys.at[k - 1, h, u], yr.at[k - 1, h, u], dev(y_=plus(y, k)), sem("y", k, h, u))

    def m0(_):
        x_load[0].wait()
        for k in (2, 1, 3):
            block = project(k).astype(BF16)
            for h in range(2):
                for u in range(2):
                    ys[k - 1, h, u] = block[:, u, :, h * 128 : h * 128 + 128]
            if k == 2:
                enter()
            for u in range(2):
                give_y(k, 0, u)
        for u in range(2):
            for k in (2, 1, 3):
                give_y(k, 1, u)
        for copy in m_load:
            copy.wait()

        @pl.when(moved)
        def _():
            send(m_v, mr_v, swapped, sem("m"), like=lambda: m_v, cond=lambda: moved)

        @pl.when(jnp.logical_not(moved))
        def _():
            mr_v[...] = m_v[...]

        block = project(0)
        for h in range(2):
            for u in range(2):
                yown[h, u] = block[:, u, :, h * 128 : h * 128 + 128]

    def z1(s):
        h, u = divmod(s, 2)
        total = yown[h, u]
        for k in (1, 3, 2):
            arrived(yr.at[k - 1, h, u], sem("y", k, h, u))
            total = total + yr[k - 1, h, u].astype(F32)
        yown[h, u] = total
        zs[h, u] = total.astype(BF16)
        for k in (2, 1, 3):
            to = plus(zl, k)
            send(zs.at[h, u, to], zr.at[h, u, k - 1], dev(zl_=to), sem("z", k, s))

    def ct(_):
        ct_load.wait()
        for k in (2, 1, 3):
            send(ct_v.at[y], ct_v.at[y], dev(y_=plus(y, k)), sem("ct", k))

    def z2(s):
        h, u = divmod(s, 2)
        total = yown[h, u, zl]
        for k in (1, 2, 3):
            arrived(zr.at[h, u, k - 1], sem("z", k, s))
            total = total + zr[h, u, k - 1].astype(F32)
        proj[h, u, zl] = total.astype(BF16)
        for k in (2, 1, 3):
            send(proj.at[h, u, zl], proj.at[h, u, zl], dev(zl_=plus(zl, k)), sem("za", k, s))

    def dt(s):
        h, u = divmod(s, 2)
        if s == 0:
            for k in (1, 2, 3):
                arrived(ct_v.at[plus(y, 4 - k)], sem("ct", k))
        for k in (1, 2, 3):
            arrived(proj.at[h, u, plus(zl, 4 - k)], sem("za", k, s))
        left = proj[h, u].reshape(256, 128)
        for b in range(4):
            right = jnp.concatenate([ct_v[b, (2 * z + u) * 64 : (2 * z + u) * 64 + 64] for z in range(4)], axis=0)
            block = lax.dot_general(left, right, (((0,), (0,)), ((), ())), preferred_element_type=F32)
            block = block.reshape(2, 2, 32, 256)
            for i in range(2):
                for cc in range(2):
                    if u == 0:
                        plow[h, cc, i, b] = block[i, cc]
                    else:
                        plow[h, cc, i, b] += block[i, cc]
        if u == 1:
            cs[h] = plow[h, other].astype(BF16)
            send(cs.at[h], cr.at[h], dev(c_=other), sem("c", h))

    def bx(h):
        arrived(cr.at[h], sem("c", h))
        total = plow[h, c] + cr[h].astype(F32)
        csum[h] = total
        xs[h] = total.astype(BF16)
        for k in (2, 1, 3):
            to = plus(x, k)

            @pl.when(lax.div(to, 2) == h)
            def _():
                send(
                    xs.at[h, lax.rem(to, 2)], xr.at[k - 1], dev(x_=to), sem("x", k),
                    like=lambda: xs.at[0, 0], cond=lambda k=k: lax.div(plus(x, k), 2) == h,
                )

    def bh(h):
        @pl.when(xh == h)
        def _():
            total = csum[h, xx]
            for k in (1, 3, 2):
                arrived(xr.at[k - 1], sem("x", k))
                total = total + xr[k - 1].astype(F32)
            xsum[...] = total
            hs[...] = total.astype(BF16)
            for k in (2, 1, 3):
                to = plus(zh, k)
                send(
                    hs.at[to], hr.at[k - 1], dev(zh_=to), sem("h", k),
                    like=lambda: hs.at[0], cond=lambda: xh == h,
                )

    def moments(m, low):
        return 0.9 * m[0] + 0.1 * low, 0.999 * m[1] + 0.001 * low * low

    def ad(h):
        @pl.when(moved & (xh == h))
        def _():
            arrived(mr_v, sem("m"))

        @pl.when(xh == h)
        def _():
            total = xsum[zh]
            for k in (1, 3, 2):
                arrived(hr.at[k - 1], sem("h", k))
                total = total + hr[k - 1].astype(F32)
            low = total / REPLICAS
            low_v[...] = low
            first, second = moments(mr_v, low)
            first_hat = first / (1.0 - 0.9**STEP)
            second_hat = second / (1.0 - 0.999**STEP)
            update = (first_hat / (jnp.sqrt(second_hat) + 1e-08)).astype(BF16)
            upd[0] = update[:, :128]
            upd[1] = update[:, 128:]
            place = need.at[y, x, c]
            at = sem("n", 0, 0, 0) + x * 2 + c
            for k in (2, 1, 3, 0):
                for same in (0, 1):
                    half = c if same else other
                    device = dev(x_=zl, c_=half, zl_=plus(zl, k))
                    index = sem("n", 1, k, same)
                    rest = dict(like=lambda: upd.at[0])
                    if k == 0 and same:

                        @pl.when(apart)
                        def _():
                            send(upd.at[c], place, device, index, at, cond=lambda: apart & (xh == h), **rest)

                        @pl.when(jnp.logical_not(apart))
                        def _():
                            need[y, x, c] = upd[c]
                    else:
                        send(upd.at[half], place, device, index, at, cond=lambda: xh == h, **rest)

        @pl.when((xh == h) & moved)
        def _():
            send(low_v, back, swapped, sem("b"), like=lambda: back, cond=lambda: (xh == h) & moved)

    def c1(h):
        for i in (2 * h, 2 * h + 1):
            for cc in range(2):

                @pl.when(jnp.logical_or(apart, jnp.logical_or(i != x, cc != c)))
                def _():
                    arrived(need.at[y, i, cc], sem("n", 0, i, cc))

        mine = need.at[y, pl.ds(2 * h, 2)]
        for k in (2, 1, 3):
            send(mine, mine, dev(y_=plus(y, k)), sem("g", k, h))

    def d(h):
        for k in (1, 3, 2):
            arrived(need.at[plus(y, 4 - k), pl.ds(2 * h, 2)], sem("g", k, h))
        if h == 1:
            w_load.wait()
        lower = [need[a, 2 * h : 2 * h + 2].reshape(128, 128) for a in range(4)]
        for r in range(0, 1024, 256):
            span = slice(r, r + 256)
            change = sum(dot(p_v[a, span, h * 128 : h * 128 + 128], lower[a]) for a in range(4))
            if h == 0:
                acc[span] = change
            else:
                ow[span] = (w_v[span].astype(F32) - 0.5 * (acc[span] + change)).astype(BF16)

    def own(_):
        @pl.when(moved)
        def _():
            arrived(back, sem("b"))

        @pl.when(jnp.logical_not(moved))
        def _():
            back[...] = low_v[...]

        o1[...], o2[...] = moments(m_v, back[...])

    for i in range(4):
        for cc in range(2):
            sem("n", 0, i, cc)
    plan = [
        (0, m0, 0), (4.7, z1, 0), (6.7, z1, 1), (6.8, ct, 0), (8.7, z1, 2), (8.9, z2, 0), (10.7, z1, 3), (10.9, z2, 1),
        (12.9, z2, 2), (14.9, z2, 3), (15.2, dt, 0), (16, dt, 1), (17.1, dt, 2), (17.5, bx, 0), (19.1, dt, 3),
        (20.5, bx, 1), (21.1, bh, 0), (24.5, bh, 1), (28, ad, 0), (32, ad, 1), (33, c1, 0), (37, c1, 1), (38, d, 0), (41, d, 1),
        (42, own, 0),
    ]
    for _, stage, index in plan:
        stage(index)

    for like, index, cond in waits:
        wait = copy_of(like(), like(), dev(c_=other), index).wait_send
        if cond is None:
            wait()
        else:
            pl.when(cond())(wait)


def local(weight, inputs, cotangent, projector, first_moment, second_moment):
    v = pltpu.VMEM
    return pl.pallas_call(
        kernel,
        out_shape=(
            jax.ShapeDtypeStruct((1024, 128), BF16),
            jax.ShapeDtypeStruct((32, 256), F32),
            jax.ShapeDtypeStruct((32, 256), F32),
        ),
        in_specs=[pl.BlockSpec(memory_space=pl.ANY)] * 6,
        out_specs=[pl.BlockSpec(memory_space=pltpu.VMEM)] * 3,
        scratch_shapes=[
            v((1024, 128), BF16),
            v((512, 1024), BF16),
            v((4, 512, 256), BF16),
            v((4, 1024, 256), BF16),
            v((2, 32, 256), F32),
            v((2, 32, 256), F32),
            v((3, 2, 2, 4, 64, 128), BF16),
            v((3, 2, 2, 4, 64, 128), BF16),
            v((2, 2, 4, 64, 128), F32),
            v((2, 2, 4, 64, 128), BF16),
            v((2, 2, 3, 64, 128), BF16),
            v((2, 2, 4, 64, 128), BF16),
            v((2, 2, 2, 4, 32, 256), F32),
            v((2, 2, 4, 32, 256), BF16),
            v((2, 2, 4, 32, 256), BF16),
            v((2, 2, 4, 32, 256), F32),
            v((2, 2, 4, 32, 256), BF16),
            v((3, 4, 32, 256), BF16),
            v((4, 32, 256), F32),
            v((4, 32, 256), BF16),
            v((3, 32, 256), BF16),
            v((32, 256), F32),
            v((32, 256), F32),
            v((2, 32, 128), BF16),
            v((4, 4, 2, 32, 128), BF16),
            v((1024, 128), F32),
            pltpu.SemaphoreType.DMA((20,)),
            pltpu.SemaphoreType.DMA((96,)),
            pltpu.SemaphoreType.DMA((96,)),
        ],
        compiler_params=pltpu.CompilerParams(
            collective_id=0, has_side_effects=True, vmem_limit_bytes=58 * 2**20
        ),
    )(weight, inputs, cotangent, projector, first_moment, second_moment)


def solution(mesh):
    placed = (
        P("tensor", "dp"),
        P("dp", "tensor"),
        P("dp", "tensor"),
        P("tensor", None),
        P("dp", "tensor"),
        P("dp", "tensor"),
    )
    return jax.shard_map(
        local,
        mesh=mesh,
        in_specs=placed,
        out_specs=(P("tensor", "dp"), P("dp", "tensor"), P("dp", "tensor")),
        check_vma=False,
    )
```

```python
import jax
import jax.numpy as jnp
from jax import lax
from jax.experimental import pallas as pl
from jax.experimental.pallas import tpu as pltpu
from jax.sharding import PartitionSpec as P

STEP = 10
REPLICAS = 32
MESH = pl.DeviceIdType.MESH
F32, BF16 = jnp.float32, jnp.bfloat16


def kernel(
    w_hbm, x_hbm, ct_hbm, p_hbm, m1_hbm, m2_hbm,
    ow, o1, o2,
    w_v, x_v, ct_v, p_v, m_v, mr_v,
    y1s, y1r, y2s, y2r, mid, yown, zs, zr, proj,
    plow, cs, cr, csum, xs, xr, xsum, hs, hr, low_v, back, upd, need, acc,
    lsem, ssem, rsem, known,
):
    dp, t = lax.axis_index("dp"), lax.axis_index("tensor")
    zh, x, c = lax.div(dp, 8), lax.rem(lax.div(dp, 2), 4), lax.rem(dp, 2)
    y, zl = lax.div(t, 4), lax.rem(t, 4)
    xh, xx = lax.div(x, 2), lax.rem(x, 2)
    other = 1 - c
    moved = zh != y
    apart = x != zl

    def plus(v, k):
        return lax.rem(v + k, 4)

    def dev(zh_=zh, x_=x, c_=c, y_=y, zl_=zl):
        return {"dp": zh_ * 8 + x_ * 2 + c_, "tensor": y_ * 4 + zl_}

    count = {"l": 0}
    ids = {}
    waits = []
    state = {"mute": False}

    def sem(*key):
        return ids.setdefault(key, len(ids))

    def load(src, dst):
        copy = pltpu.make_async_copy(src, dst, lsem.at[count["l"]])
        count["l"] += 1
        copy.start()
        return copy

    def copy_of(src, dst, device, index, at=None):
        return pltpu.make_async_remote_copy(
            src_ref=src, dst_ref=dst, send_sem=ssem.at[index],
            recv_sem=rsem.at[index if at is None else at], device_id=device, device_id_type=MESH,
        )

    def send(src, dst, device, index, at=None, like=None, cond=None):
        if not state["mute"]:
            copy_of(src, dst, device, index, at).start()
            waits.append((like or (lambda: src), index, cond))

    def arrived(dst, index):
        copy_of(dst, dst, dev(c_=other), index).wait_recv()

    def dot(a, b):
        return jnp.dot(a, b, preferred_element_type=F32)

    p_load, x_load = {}, []
    for k in (2, 1, 3, 0):
        b = plus(y, k)
        p_load[k] = load(p_hbm.at[:, pl.ds(pl.multiple_of(b * 256, 256), 256)], p_v.at[b])
        if k == 2:
            x_load.append(load(x_hbm, x_v))
    m_load = [load(m1_hbm, m_v.at[0]), load(m2_hbm, m_v.at[1])]
    ct_load = load(ct_hbm, ct_v.at[y])
    w_load = load(w_hbm, w_v)

    barrier = pltpu.get_barrier_semaphore()

    def signal(device):
        pl.semaphore_signal(barrier, inc=1, device_id=device, device_id_type=MESH)

    swapped = dev(zh_=y, y_=zh)
    around = [dev(zh_=plus(zh, k)) for k in (1, 3)]
    y_up, y_down = dev(y_=plus(y, 1)), dev(y_=plus(y, 3))
    near = [y_up, y_down, dev(c_=other)]
    near += [dev(zl_=plus(zl, k)) for k in (1, 2, 3)]
    near += [dev(x_=plus(x, k)) for k in (1, 2, 3)]
    near += around
    for device in near:
        signal(device)

    def enter():
        pl.semaphore_wait(barrier, len(near))
        spread(0)

    def spread(step):
        for i in range(2):
            pl.semaphore_signal(known.at[step, i], inc=1, device_id=around[i], device_id_type=MESH)

    def heard(step):
        for i in range(2):
            pl.semaphore_wait(known.at[step, i], 1)

    def project(k):
        p_load[k].wait()
        return dot(x_v[...], p_v[plus(y, k)]).reshape(4, 2, 64, 256)

    def cut(block, h, u):
        return block[:, u, :, h * 128 : h * 128 + 128]

    def m0(_):
        x_load[0].wait()
        block = project(2).astype(BF16)
        for h in range(2):
            for u in range(2):
                y1s[h, u] = cut(block, h, u)
        enter()
        for h in range(2):
            for u in range(2):
                send(y1s.at[h, u, pl.ds(0, 2)], y1r.at[0, h, u], y_up, sem("y1", 0, h, u))
                send(y1s.at[h, u, pl.ds(2, 2)], y1r.at[1, h, u], y_down, sem("y1", 1, h, u))
        for i, k in enumerate((1, 3)):
            block = project(k)
            for h in range(2):
                for u in range(2):
                    mid[i, h, u] = cut(block, h, u)
        block = project(0)
        for h in range(2):
            for u in range(2):
                yown[h, u] = cut(block, h, u)

    def y1(s):
        h, u = divmod(s, 2)
        for i, device in enumerate((y_up, y_down)):
            added, rest = (pl.ds(0, 2), pl.ds(2, 2)) if i == 0 else (pl.ds(2, 2), pl.ds(0, 2))
            y2s[i, h, u, rest] = mid[i, h, u, rest].astype(BF16)
            arrived(y1r.at[i, h, u], sem("y1", i, h, u))
            y2s[i, h, u, added] = (mid[i, h, u, added] + y1r[i, h, u].astype(F32)).astype(BF16)
            send(y2s.at[i, h, u], y2r.at[i, h, u], device, sem("y2", i, h, u))

    def hop(_):
        heard(0)
        spread(1)

    def mo(_):
        heard(1)
        for copy in m_load:
            copy.wait()

        @pl.when(moved)
        def _():
            send(m_v, mr_v, swapped, sem("m"), like=lambda: m_v, cond=lambda: moved)

        @pl.when(jnp.logical_not(moved))
        def _():
            mr_v[...] = m_v[...]

    def z1(s):
        h, u = divmod(s, 2)
        total = yown[h, u]
        for i in range(2):
            arrived(y2r.at[i, h, u], sem("y2", i, h, u))
            total = total + y2r[i, h, u].astype(F32)
        yown[h, u] = total
        zs[h, u] = total.astype(BF16)
        for k in (2, 1, 3):
            to = plus(zl, k)
            send(zs.at[h, u, to], zr.at[h, u, k - 1], dev(zl_=to), sem("z", k, s))

    def ct(_):
        ct_load.wait()
        send(ct_v.at[y], ct_v.at[y], y_up, sem("ct", 0))
        send(ct_v.at[y], ct_v.at[y], y_down, sem("ct", 1))

    def cf(_):
        up, down = plus(y, 3), plus(y, 1)
        arrived(ct_v.at[up], sem("ct", 0))
        first = ct_v.at[up, pl.ds(0, 256)]
        send(first, first, y_up, sem("cf", 0))
        arrived(ct_v.at[down], sem("ct", 1))
        second = ct_v.at[down, pl.ds(256, 256)]
        send(second, second, y_down, sem("cf", 1))

    def z2(s):
        h, u = divmod(s, 2)
        total = yown[h, u, zl]
        for k in (1, 2, 3):
            arrived(zr.at[h, u, k - 1], sem("z", k, s))
            total = total + zr[h, u, k - 1].astype(F32)
        proj[h, u, zl] = total.astype(BF16)
        for k in (2, 1, 3):
            send(proj.at[h, u, zl], proj.at[h, u, zl], dev(zl_=plus(zl, k)), sem("za", k, s))

    def dt(s):
        h, u = divmod(s, 2)
        if s == 0:
            arrived(ct_v.at[plus(y, 2), pl.ds(0, 256)], sem("cf", 0))
            arrived(ct_v.at[plus(y, 2), pl.ds(256, 256)], sem("cf", 1))
        for k in (1, 2, 3):
            arrived(proj.at[h, u, plus(zl, 4 - k)], sem("za", k, s))
        left = proj[h, u].reshape(256, 128)
        for b in range(4):
            right = jnp.concatenate([ct_v[b, (2 * z + u) * 64 : (2 * z + u) * 64 + 64] for z in range(4)], axis=0)
            block = lax.dot_general(left, right, (((0,), (0,)), ((), ())), preferred_element_type=F32)
            block = block.reshape(2, 2, 32, 256)
            for i in range(2):
                for cc in range(2):
                    if u == 0:
                        plow[h, cc, i, b] = block[i, cc]
                    else:
                        plow[h, cc, i, b] += block[i, cc]
        if u == 1:
            cs[h] = plow[h, other].astype(BF16)
            send(cs.at[h], cr.at[h], dev(c_=other), sem("c", h))

    def bx(h):
        arrived(cr.at[h], sem("c", h))
        total = plow[h, c] + cr[h].astype(F32)
        csum[h] = total
        xs[h] = total.astype(BF16)
        for k in (2, 1, 3):
            to = plus(x, k)

            @pl.when(lax.div(to, 2) == h)
            def _():
                send(
                    xs.at[h, lax.rem(to, 2)], xr.at[k - 1], dev(x_=to), sem("x", k),
                    like=lambda: xs.at[0, 0], cond=lambda k=k: lax.div(plus(x, k), 2) == h,
                )

    def bh(h):
        @pl.when(xh == h)
        def _():
            total = csum[h, xx]
            for k in (1, 3, 2):
                arrived(xr.at[k - 1], sem("x", k))
                total = total + xr[k - 1].astype(F32)
            xsum[...] = total
            hs[...] = total.astype(BF16)
            for k in (2, 1, 3):
                to = plus(zh, k)
                send(
                    hs.at[to], hr.at[k - 1], dev(zh_=to), sem("h", k),
                    like=lambda: hs.at[0], cond=lambda: xh == h,
                )

    def moments(m, low):
        return 0.9 * m[0] + 0.1 * low, 0.999 * m[1] + 0.001 * low * low

    def ad(h):
        @pl.when(moved & (xh == h))
        def _():
            arrived(mr_v, sem("m"))

        @pl.when(xh == h)
        def _():
            total = xsum[zh]
            for k in (1, 3, 2):
                arrived(hr.at[k - 1], sem("h", k))
                total = total + hr[k - 1].astype(F32)
            low = total / REPLICAS
            low_v[...] = low
            first, second = moments(mr_v, low)
            first_hat = first / (1.0 - 0.9**STEP)
            second_hat = second / (1.0 - 0.999**STEP)
            update = (first_hat / (jnp.sqrt(second_hat) + 1e-08)).astype(BF16)
            upd[0] = update[:, :128]
            upd[1] = update[:, 128:]
            place = need.at[y, x, c]
            at = sem("n", 0, 0, 0) + x * 2 + c
            for k in (2, 1, 3, 0):
                for same in (0, 1):
                    half = c if same else other
                    device = dev(x_=zl, c_=half, zl_=plus(zl, k))
                    index = sem("n", 1, k, same)
                    rest = dict(like=lambda: upd.at[0])
                    if k == 0 and same:

                        @pl.when(apart)
                        def _():
                            send(upd.at[c], place, device, index, at, cond=lambda: apart & (xh == h), **rest)

                        @pl.when(jnp.logical_not(apart))
                        def _():
                            need[y, x, c] = upd[c]
                    else:
                        send(upd.at[half], place, device, index, at, cond=lambda: xh == h, **rest)

        @pl.when((xh == h) & moved)
        def _():
            send(low_v, back, swapped, sem("b"), like=lambda: back, cond=lambda: (xh == h) & moved)

    def c1(h):
        for i in (2 * h, 2 * h + 1):
            for cc in range(2):

                @pl.when(jnp.logical_or(apart, jnp.logical_or(i != x, cc != c)))
                def _():
                    arrived(need.at[y, i, cc], sem("n", 0, i, cc))

        mine = need.at[y, pl.ds(2 * h, 2)]
        for k in (2, 1, 3):
            send(mine, mine, dev(y_=plus(y, k)), sem("g", k, h))

    def d(h):
        for k in (1, 3, 2):
            arrived(need.at[plus(y, 4 - k), pl.ds(2 * h, 2)], sem("g", k, h))
        if h == 1:
            w_load.wait()
        lower = [need[a, 2 * h : 2 * h + 2].reshape(128, 128) for a in range(4)]
        for r in range(0, 1024, 256):
            span = slice(r, r + 256)
            change = sum(dot(p_v[a, span, h * 128 : h * 128 + 128], lower[a]) for a in range(4))
            if h == 0:
                acc[span] = change
            else:
                ow[span] = (w_v[span].astype(F32) - 0.5 * (acc[span] + change)).astype(BF16)

    def own(_):
        @pl.when(moved)
        def _():
            arrived(back, sem("b"))

        @pl.when(jnp.logical_not(moved))
        def _():
            back[...] = low_v[...]

        o1[...], o2[...] = moments(m_v, back[...])

    for i in range(4):
        for cc in range(2):
            sem("n", 0, i, cc)
    plan = [(m0, 0)] + [(y1, s) for s in range(4)]
    plan += [(z1, 0), (z1, 1), (ct, 0), (z1, 2), (z1, 3)]
    plan += [(z2, s) for s in range(4)] + [(hop, 0), (cf, 0)] + [(dt, s) for s in range(4)]
    plan += [(bx, 0), (bx, 1), (mo, 0)]
    plan += [(stage, h) for stage in (bh, ad, c1, d) for h in range(2)]
    plan += [(own, 0)]
    for stage, index in plan:
        stage(index)

    for like, index, cond in waits:
        wait = copy_of(like(), like(), dev(c_=other), index).wait_send
        if cond is None:
            wait()
        else:
            pl.when(cond())(wait)


def leave(a, b, c, oa, ob, oc):
    oa[...] = a[...]
    ob[...] = b[...]
    oc[...] = c[...]


def local(weight, inputs, cotangent, projector, first_moment, second_moment):
    v = pltpu.VMEM
    shapes = (
        jax.ShapeDtypeStruct((1024, 128), BF16),
        jax.ShapeDtypeStruct((32, 256), F32),
        jax.ShapeDtypeStruct((32, 256), F32),
    )
    results = pl.pallas_call(
        kernel,
        out_shape=shapes,
        in_specs=[pl.BlockSpec(memory_space=pl.ANY)] * 6,
        out_specs=[pl.BlockSpec(memory_space=pltpu.VMEM)] * 3,
        scratch_shapes=[
            v((1024, 128), BF16),
            v((512, 1024), BF16),
            v((4, 512, 256), BF16),
            v((4, 1024, 256), BF16),
            v((2, 32, 256), F32),
            v((2, 32, 256), F32),
            v((2, 2, 4, 64, 128), BF16),
            v((2, 2, 2, 2, 64, 128), BF16),
            v((2, 2, 2, 4, 64, 128), BF16),
            v((2, 2, 2, 4, 64, 128), BF16),
            v((2, 2, 2, 4, 64, 128), F32),
            v((2, 2, 4, 64, 128), F32),
            v((2, 2, 4, 64, 128), BF16),
            v((2, 2, 3, 64, 128), BF16),
            v((2, 2, 4, 64, 128), BF16),
            v((2, 2, 2, 4, 32, 256), F32),
            v((2, 2, 4, 32, 256), BF16),
            v((2, 2, 4, 32, 256), BF16),
            v((2, 2, 4, 32, 256), F32),
            v((2, 2, 4, 32, 256), BF16),
            v((3, 4, 32, 256), BF16),
            v((4, 32, 256), F32),
            v((4, 32, 256), BF16),
            v((3, 32, 256), BF16),
            v((32, 256), F32),
            v((32, 256), F32),
            v((2, 32, 128), BF16),
            v((4, 4, 2, 32, 128), BF16),
            v((1024, 128), F32),
            pltpu.SemaphoreType.DMA((20,)),
            pltpu.SemaphoreType.DMA((96,)),
            pltpu.SemaphoreType.DMA((96,)),
            pltpu.SemaphoreType.REGULAR((2, 2)),
        ],
        compiler_params=pltpu.CompilerParams(
            collective_id=0, has_side_effects=True, vmem_limit_bytes=58 * 2**20
        ),
    )(weight, inputs, cotangent, projector, first_moment, second_moment)
    return pl.pallas_call(
        leave,
        out_shape=shapes,
        in_specs=[pl.BlockSpec(memory_space=pltpu.VMEM)] * 3,
        out_specs=[pl.BlockSpec(memory_space=pltpu.VMEM)] * 3,
        compiler_params=pltpu.CompilerParams(vmem_limit_bytes=58 * 2**20),
    )(*results)


def solution(mesh):
    placed = (
        P("tensor", "dp"),
        P("dp", "tensor"),
        P("dp", "tensor"),
        P("tensor", None),
        P("dp", "tensor"),
        P("dp", "tensor"),
    )
    return jax.shard_map(
        local,
        mesh=mesh,
        in_specs=placed,
        out_specs=(P("tensor", "dp"), P("dp", "tensor"), P("dp", "tensor")),
        check_vma=False,
    )
```

```python
import jax
import jax.numpy as jnp
from jax import lax
from jax.experimental import pallas as pl
from jax.experimental.pallas import tpu as pltpu
from jax.sharding import PartitionSpec as P

STEP = 10
REPLICAS = 32
MESH = pl.DeviceIdType.MESH
F32, BF16 = jnp.float32, jnp.bfloat16


def kernel(
    w_hbm, x_hbm, ct_hbm, p_hbm, m1_hbm, m2_hbm,
    ow, o1, o2,
    w_v, x_v, ct_v, p_v, m_v, mr_v,
    y1s, y1r, y2s, y2r, mid, yown, zs, zr, proj,
    plow, cs, cr, csum, xs, xr, xsum, hs, hr, low_v, back, upd, need, acc,
    lsem, ssem, rsem, known,
):
    dp, t = lax.axis_index("dp"), lax.axis_index("tensor")
    zh, x, c = lax.div(dp, 8), lax.rem(lax.div(dp, 2), 4), lax.rem(dp, 2)
    y, zl = lax.div(t, 4), lax.rem(t, 4)
    xh, xx = lax.div(x, 2), lax.rem(x, 2)
    other = 1 - c
    moved = zh != y
    apart = x != zl

    def plus(v, k):
        return lax.rem(v + k, 4)

    def dev(zh_=zh, x_=x, c_=c, y_=y, zl_=zl):
        return {"dp": zh_ * 8 + x_ * 2 + c_, "tensor": y_ * 4 + zl_}

    count = {"l": 0}
    ids = {}
    waits = []
    state = {"mute": False}

    def sem(*key):
        return ids.setdefault(key, len(ids))

    def load(src, dst):
        copy = pltpu.make_async_copy(src, dst, lsem.at[count["l"]])
        count["l"] += 1
        copy.start()
        return copy

    def copy_of(src, dst, device, index, at=None):
        return pltpu.make_async_remote_copy(
            src_ref=src, dst_ref=dst, send_sem=ssem.at[index],
            recv_sem=rsem.at[index if at is None else at], device_id=device, device_id_type=MESH,
        )

    def send(src, dst, device, index, at=None, like=None, cond=None):
        if not state["mute"]:
            copy_of(src, dst, device, index, at).start()
            waits.append((like or (lambda: src), index, cond))

    def arrived(dst, index):
        copy_of(dst, dst, dev(c_=other), index).wait_recv()

    def dot(a, b):
        return jnp.dot(a, b, preferred_element_type=F32)

    barrier = pltpu.get_barrier_semaphore()

    def signal(device):
        pl.semaphore_signal(barrier, inc=1, device_id=device, device_id_type=MESH)

    swapped = dev(zh_=y, y_=zh)
    around = [dev(zh_=plus(zh, k)) for k in (1, 3)]
    y_up, y_down = dev(y_=plus(y, 1)), dev(y_=plus(y, 3))
    near = [y_up, y_down, dev(c_=other)]
    near += [dev(zl_=plus(zl, k)) for k in (1, 2, 3)]
    near += [dev(x_=plus(x, k)) for k in (1, 2, 3)]
    near += around
    for device in near:
        signal(device)

    p_load, x_load = {}, []
    for k in (2, 1, 3, 0):
        b = plus(y, k)
        p_load[k] = load(p_hbm.at[:, pl.ds(pl.multiple_of(b * 256, 256), 256)], p_v.at[b])
        if k == 2:
            x_load.append(load(x_hbm, x_v))
    m_load = [load(m1_hbm, m_v.at[0]), load(m2_hbm, m_v.at[1])]
    ct_load = load(ct_hbm, ct_v.at[y])
    w_load = load(w_hbm, w_v)

    def enter():
        pl.semaphore_wait(barrier, len(near))
        spread(0)

    def spread(step):
        for i in range(2):
            pl.semaphore_signal(known.at[step, i], inc=1, device_id=around[i], device_id_type=MESH)

    def heard(step):
        for i in range(2):
            pl.semaphore_wait(known.at[step, i], 1)

    def project(k):
        p_load[k].wait()
        return dot(x_v[...], p_v[plus(y, k)]).reshape(4, 2, 64, 256)

    def cut(block, h, u):
        return block[:, u, :, h * 128 : h * 128 + 128]

    def m0(_):
        x_load[0].wait()
        block = project(2).astype(BF16)
        for h in range(2):
            for u in range(2):
                y1s[h, u] = cut(block, h, u)
        enter()
        for h in range(2):
            for u in range(2):
                send(y1s.at[h, u, pl.ds(0, 2)], y1r.at[0, h, u], y_up, sem("y1", 0, h, u))
                send(y1s.at[h, u, pl.ds(2, 2)], y1r.at[1, h, u], y_down, sem("y1", 1, h, u))
        for i, k in enumerate((1, 3)):
            block = project(k)
            for h in range(2):
                for u in range(2):
                    mid[i, h, u] = cut(block, h, u)
        block = project(0)
        for h in range(2):
            for u in range(2):
                yown[h, u] = cut(block, h, u)

    def y1(s):
        h, u = divmod(s, 2)
        for i, device in enumerate((y_up, y_down)):
            added, rest = (pl.ds(0, 2), pl.ds(2, 2)) if i == 0 else (pl.ds(2, 2), pl.ds(0, 2))
            y2s[i, h, u, rest] = mid[i, h, u, rest].astype(BF16)
            arrived(y1r.at[i, h, u], sem("y1", i, h, u))
            y2s[i, h, u, added] = (mid[i, h, u, added] + y1r[i, h, u].astype(F32)).astype(BF16)
            send(y2s.at[i, h, u], y2r.at[i, h, u], device, sem("y2", i, h, u))

    def hop(_):
        heard(0)
        spread(1)

    def mo(_):
        heard(1)
        for copy in m_load:
            copy.wait()

        @pl.when(moved)
        def _():
            send(m_v, mr_v, swapped, sem("m"), like=lambda: m_v, cond=lambda: moved)

        @pl.when(jnp.logical_not(moved))
        def _():
            mr_v[...] = m_v[...]

    def z1(s):
        h, u = divmod(s, 2)
        total = yown[h, u]
        for i in range(2):
            arrived(y2r.at[i, h, u], sem("y2", i, h, u))
            total = total + y2r[i, h, u].astype(F32)
        yown[h, u] = total
        zs[h, u] = total.astype(BF16)
        for k in (2, 1, 3):
            to = plus(zl, k)
            send(zs.at[h, u, to], zr.at[h, u, k - 1], dev(zl_=to), sem("z", k, s))

    def ca(_):
        ct_load.wait()
        for i, device in enumerate((y_up, y_down)):
            part = ct_v.at[y, pl.ds(i * 256, 256)]
            send(part, part, device, sem("ca", i))

    def cb(_):
        for i, device in enumerate((y_up, y_down)):
            part = ct_v.at[y, pl.ds(256 - i * 256, 256)]
            send(part, part, device, sem("cb", i))

    def cf(_):
        for i, device in enumerate((y_up, y_down)):
            part = ct_v.at[plus(y, 3 - 2 * i), pl.ds(i * 256, 256)]
            arrived(part, sem("ca", i))
            send(part, part, device, sem("cf", i))

    def z2(s):
        h, u = divmod(s, 2)
        total = yown[h, u, zl]
        for k in (1, 2, 3):
            arrived(zr.at[h, u, k - 1], sem("z", k, s))
            total = total + zr[h, u, k - 1].astype(F32)
        proj[h, u, zl] = total.astype(BF16)
        for k in (2, 1, 3):
            send(proj.at[h, u, zl], proj.at[h, u, zl], dev(zl_=plus(zl, k)), sem("za", k, s))

    def dt(s):
        h, u = divmod(s, 2)
        if s == 0:
            for i in range(2):
                arrived(ct_v.at[plus(y, 3 - 2 * i), pl.ds(256 - i * 256, 256)], sem("cb", i))
                arrived(ct_v.at[plus(y, 2), pl.ds(i * 256, 256)], sem("cf", i))
        for k in (1, 2, 3):
            arrived(proj.at[h, u, plus(zl, 4 - k)], sem("za", k, s))
        left = proj[h, u].reshape(256, 128)
        for b in range(4):
            right = jnp.concatenate([ct_v[b, (2 * z + u) * 64 : (2 * z + u) * 64 + 64] for z in range(4)], axis=0)
            block = lax.dot_general(left, right, (((0,), (0,)), ((), ())), preferred_element_type=F32)
            block = block.reshape(2, 2, 32, 256)
            for i in range(2):
                for cc in range(2):
                    if u == 0:
                        plow[h, cc, i, b] = block[i, cc]
                    else:
                        plow[h, cc, i, b] += block[i, cc]
        if u == 1:
            cs[h] = plow[h, other].astype(BF16)
            send(cs.at[h], cr.at[h], dev(c_=other), sem("c", h))

    def bx(h):
        arrived(cr.at[h], sem("c", h))
        total = plow[h, c] + cr[h].astype(F32)
        csum[h] = total
        xs[h] = total.astype(BF16)
        for k in (2, 1, 3):
            to = plus(x, k)

            @pl.when(lax.div(to, 2) == h)
            def _():
                send(
                    xs.at[h, lax.rem(to, 2)], xr.at[k - 1], dev(x_=to), sem("x", k),
                    like=lambda: xs.at[0, 0], cond=lambda k=k: lax.div(plus(x, k), 2) == h,
                )

    def bh(h):
        @pl.when(xh == h)
        def _():
            total = csum[h, xx]
            for k in (1, 3, 2):
                arrived(xr.at[k - 1], sem("x", k))
                total = total + xr[k - 1].astype(F32)
            xsum[...] = total
            hs[...] = total.astype(BF16)
            for k in (2, 1, 3):
                to = plus(zh, k)
                send(
                    hs.at[to], hr.at[k - 1], dev(zh_=to), sem("h", k),
                    like=lambda: hs.at[0], cond=lambda: xh == h,
                )

    def moments(m, low):
        return 0.9 * m[0] + 0.1 * low, 0.999 * m[1] + 0.001 * low * low

    def ad(h):
        @pl.when(moved & (xh == h))
        def _():
            arrived(mr_v, sem("m"))

        @pl.when(xh == h)
        def _():
            total = xsum[zh]
            for k in (1, 3, 2):
                arrived(hr.at[k - 1], sem("h", k))
                total = total + hr[k - 1].astype(F32)
            low = total / REPLICAS
            low_v[...] = low
            first, second = moments(mr_v, low)
            first_hat = first / (1.0 - 0.9**STEP)
            second_hat = second / (1.0 - 0.999**STEP)
            update = (first_hat / (jnp.sqrt(second_hat) + 1e-08)).astype(BF16)
            upd[0] = update[:, :128]
            upd[1] = update[:, 128:]
            place = need.at[y, x, c]
            at = sem("n", 0, 0, 0) + x * 2 + c
            for k in (2, 1, 3, 0):
                for same in (0, 1):
                    half = c if same else other
                    device = dev(x_=zl, c_=half, zl_=plus(zl, k))
                    index = sem("n", 1, k, same)
                    rest = dict(like=lambda: upd.at[0])
                    if k == 0 and same:

                        @pl.when(apart)
                        def _():
                            send(upd.at[c], place, device, index, at, cond=lambda: apart & (xh == h), **rest)

                        @pl.when(jnp.logical_not(apart))
                        def _():
                            need[y, x, c] = upd[c]
                    else:
                        send(upd.at[half], place, device, index, at, cond=lambda: xh == h, **rest)

        @pl.when((xh == h) & moved)
        def _():
            send(low_v, back, swapped, sem("b"), like=lambda: back, cond=lambda: (xh == h) & moved)

    def c1(h):
        for i in (2 * h, 2 * h + 1):
            for cc in range(2):

                @pl.when(jnp.logical_or(apart, jnp.logical_or(i != x, cc != c)))
                def _():
                    arrived(need.at[y, i, cc], sem("n", 0, i, cc))

        mine = need.at[y, pl.ds(2 * h, 2)]
        for k in (2, 1, 3):
            send(mine, mine, dev(y_=plus(y, k)), sem("g", k, h))

    def d(h):
        for k in (1, 3, 2):
            arrived(need.at[plus(y, 4 - k), pl.ds(2 * h, 2)], sem("g", k, h))
        if h == 1:
            w_load.wait()
        lower = [need[a, 2 * h : 2 * h + 2].reshape(128, 128) for a in range(4)]
        for r in range(0, 1024, 256):
            span = slice(r, r + 256)
            change = sum(dot(p_v[a, span, h * 128 : h * 128 + 128], lower[a]) for a in range(4))
            if h == 0:
                acc[span] = change
            else:
                ow[span] = (w_v[span].astype(F32) - 0.5 * (acc[span] + change)).astype(BF16)

    def own(_):
        @pl.when(moved)
        def _():
            arrived(back, sem("b"))

        @pl.when(jnp.logical_not(moved))
        def _():
            back[...] = low_v[...]

        o1[...], o2[...] = moments(m_v, back[...])

    for i in range(4):
        for cc in range(2):
            sem("n", 0, i, cc)
    plan = [(m0, 0)] + [(y1, s) for s in range(4)]
    plan += [(z1, 0), (ca, 0), (z1, 1), (cb, 0), (z1, 2), (z1, 3), (hop, 0), (cf, 0)]
    plan += [(z2, s) for s in range(4)] + [(dt, s) for s in range(4)] + [(mo, 0), (bx, 0), (bx, 1)]
    plan += [(stage, h) for stage in (bh, ad, c1, d) for h in range(2)]
    plan += [(own, 0)]

    for stage, index in plan:
        stage(index)

    for like, index, cond in waits:
        wait = copy_of(like(), like(), dev(c_=other), index).wait_send
        if cond is None:
            wait()
        else:
            pl.when(cond())(wait)


def leave(a, b, c, oa, ob, oc):
    oa[...] = a[...]
    ob[...] = b[...]
    oc[...] = c[...]


def local(weight, inputs, cotangent, projector, first_moment, second_moment):
    v = pltpu.VMEM
    shapes = (
        jax.ShapeDtypeStruct((1024, 128), BF16),
        jax.ShapeDtypeStruct((32, 256), F32),
        jax.ShapeDtypeStruct((32, 256), F32),
    )
    results = pl.pallas_call(
        kernel,
        out_shape=shapes,
        in_specs=[pl.BlockSpec(memory_space=pl.ANY)] * 6,
        out_specs=[pl.BlockSpec(memory_space=pltpu.VMEM)] * 3,
        scratch_shapes=[
            v((1024, 128), BF16),
            v((512, 1024), BF16),
            v((4, 512, 256), BF16),
            v((4, 1024, 256), BF16),
            v((2, 32, 256), F32),
            v((2, 32, 256), F32),
            v((2, 2, 4, 64, 128), BF16),
            v((2, 2, 2, 2, 64, 128), BF16),
            v((2, 2, 2, 4, 64, 128), BF16),
            v((2, 2, 2, 4, 64, 128), BF16),
            v((2, 2, 2, 4, 64, 128), F32),
            v((2, 2, 4, 64, 128), F32),
            v((2, 2, 4, 64, 128), BF16),
            v((2, 2, 3, 64, 128), BF16),
            v((2, 2, 4, 64, 128), BF16),
            v((2, 2, 2, 4, 32, 256), F32),
            v((2, 2, 4, 32, 256), BF16),
            v((2, 2, 4, 32, 256), BF16),
            v((2, 2, 4, 32, 256), F32),
            v((2, 2, 4, 32, 256), BF16),
            v((3, 4, 32, 256), BF16),
            v((4, 32, 256), F32),
            v((4, 32, 256), BF16),
            v((3, 32, 256), BF16),
            v((32, 256), F32),
            v((32, 256), F32),
            v((2, 32, 128), BF16),
            v((4, 4, 2, 32, 128), BF16),
            v((1024, 128), F32),
            pltpu.SemaphoreType.DMA((20,)),
            pltpu.SemaphoreType.DMA((96,)),
            pltpu.SemaphoreType.DMA((96,)),
            pltpu.SemaphoreType.REGULAR((2, 2)),
        ],
        compiler_params=pltpu.CompilerParams(
            collective_id=0, has_side_effects=True, vmem_limit_bytes=58 * 2**20
        ),
    )(weight, inputs, cotangent, projector, first_moment, second_moment)
    return pl.pallas_call(
        leave,
        out_shape=shapes,
        in_specs=[pl.BlockSpec(memory_space=pltpu.VMEM)] * 3,
        out_specs=[pl.BlockSpec(memory_space=pltpu.VMEM)] * 3,
        compiler_params=pltpu.CompilerParams(vmem_limit_bytes=58 * 2**20),
    )(*results)


def solution(mesh):
    placed = (
        P("tensor", "dp"),
        P("dp", "tensor"),
        P("dp", "tensor"),
        P("tensor", None),
        P("dp", "tensor"),
        P("dp", "tensor"),
    )
    return jax.shard_map(
        local,
        mesh=mesh,
        in_specs=placed,
        out_specs=(P("tensor", "dp"), P("dp", "tensor"), P("dp", "tensor")),
        check_vma=False,
    )
```

```python
import jax
import jax.numpy as jnp
from jax import lax
from jax.experimental import pallas as pl
from jax.experimental.pallas import tpu as pltpu
from jax.sharding import PartitionSpec as P

STEP = 10
REPLICAS = 32
MESH = pl.DeviceIdType.MESH
F32, BF16 = jnp.float32, jnp.bfloat16


def kernel(
    w_hbm, x_hbm, ct_hbm, p_hbm, m1_hbm, m2_hbm,
    ow, o1, o2,
    w_v, x_v, ct_v, p_v, m_v, mr_v,
    y1s, y1r, y2s, y2r, mid, yown, zs, zr, proj,
    plow, cs, cr, csum, xs, xr, xsum, hs, hr, low_v, back, upd, need, acc, nw_v, nm_v,
    lsem, ssem, rsem, known,
):
    dp, t = lax.axis_index("dp"), lax.axis_index("tensor")
    zh, x, c = lax.div(dp, 8), lax.rem(lax.div(dp, 2), 4), lax.rem(dp, 2)
    y, zl = lax.div(t, 4), lax.rem(t, 4)
    xh, xx = lax.div(x, 2), lax.rem(x, 2)
    other = 1 - c
    moved = zh != y
    apart = x != zl

    def plus(v, k):
        return lax.rem(v + k, 4)

    def dev(zh_=zh, x_=x, c_=c, y_=y, zl_=zl):
        return {"dp": zh_ * 8 + x_ * 2 + c_, "tensor": y_ * 4 + zl_}

    count = {"l": 0}
    ids = {}
    waits = []
    leaving = []
    state = {"mute": False}

    def sem(*key):
        return ids.setdefault(key, len(ids))

    def load(src, dst):
        copy = pltpu.make_async_copy(src, dst, lsem.at[count["l"]])
        count["l"] += 1
        copy.start()
        return copy

    def copy_of(src, dst, device, index, at=None):
        return pltpu.make_async_remote_copy(
            src_ref=src, dst_ref=dst, send_sem=ssem.at[index],
            recv_sem=rsem.at[index if at is None else at], device_id=device, device_id_type=MESH,
        )

    def send(src, dst, device, index, at=None, like=None, cond=None):
        if not state["mute"]:
            copy_of(src, dst, device, index, at).start()
            waits.append((like or (lambda: src), index, cond))

    def arrived(dst, index):
        copy_of(dst, dst, dev(c_=other), index).wait_recv()

    def dot(a, b):
        return jnp.dot(a, b, preferred_element_type=F32)

    barrier = pltpu.get_barrier_semaphore()

    def signal(device):
        pl.semaphore_signal(barrier, inc=1, device_id=device, device_id_type=MESH)

    swapped = dev(zh_=y, y_=zh)
    around = [dev(zh_=plus(zh, k)) for k in (1, 3)]
    y_up, y_down = dev(y_=plus(y, 1)), dev(y_=plus(y, 3))
    near = [y_up, y_down, dev(c_=other)]
    near += [dev(zl_=plus(zl, k)) for k in (1, 2, 3)]
    near += [dev(x_=plus(x, k)) for k in (1, 2, 3)]
    near += around
    for device in near:
        signal(device)

    p_load, x_load = {}, []
    for k in (2, 1, 3, 0):
        b = plus(y, k)
        p_load[k] = load(p_hbm.at[:, pl.ds(pl.multiple_of(b * 256, 256), 256)], p_v.at[b])
        if k == 2:
            x_load.append(load(x_hbm, x_v))
    m_load = [load(m1_hbm, m_v.at[0]), load(m2_hbm, m_v.at[1])]
    ct_load = load(ct_hbm, ct_v.at[y])
    w_load = load(w_hbm, w_v)

    def enter():
        pl.semaphore_wait(barrier, len(near))
        spread(0)

    def spread(step):
        for i in range(2):
            pl.semaphore_signal(known.at[step, i], inc=1, device_id=around[i], device_id_type=MESH)

    def heard(step):
        for i in range(2):
            pl.semaphore_wait(known.at[step, i], 1)

    def project(k):
        p_load[k].wait()
        return dot(x_v[...], p_v[plus(y, k)]).reshape(4, 2, 64, 256)

    def cut(block, h, u):
        return block[:, u, :, h * 128 : h * 128 + 128]

    def m0(_):
        x_load[0].wait()
        block = project(2).astype(BF16)
        for h in range(2):
            for u in range(2):
                y1s[h, u] = cut(block, h, u)
        enter()
        for h in range(2):
            for u in range(2):
                send(y1s.at[h, u, pl.ds(0, 2)], y1r.at[0, h, u], y_up, sem("y1", 0, h, u))
                send(y1s.at[h, u, pl.ds(2, 2)], y1r.at[1, h, u], y_down, sem("y1", 1, h, u))
        for i, k in enumerate((1, 3)):
            block = project(k)
            for h in range(2):
                for u in range(2):
                    mid[i, h, u] = cut(block, h, u)
        block = project(0)
        for h in range(2):
            for u in range(2):
                yown[h, u] = cut(block, h, u)

    def y1(s):
        h, u = divmod(s, 2)
        for i, device in enumerate((y_up, y_down)):
            added, rest = (pl.ds(0, 2), pl.ds(2, 2)) if i == 0 else (pl.ds(2, 2), pl.ds(0, 2))
            y2s[i, h, u, rest] = mid[i, h, u, rest].astype(BF16)
            arrived(y1r.at[i, h, u], sem("y1", i, h, u))
            y2s[i, h, u, added] = (mid[i, h, u, added] + y1r[i, h, u].astype(F32)).astype(BF16)
            send(y2s.at[i, h, u], y2r.at[i, h, u], device, sem("y2", i, h, u))

    def hop(_):
        heard(0)
        spread(1)

    def mo(_):
        heard(1)
        for copy in m_load:
            copy.wait()

        @pl.when(moved)
        def _():
            send(m_v, mr_v, swapped, sem("m"), like=lambda: m_v, cond=lambda: moved)

        @pl.when(jnp.logical_not(moved))
        def _():
            mr_v[...] = m_v[...]

    def z1(s):
        h, u = divmod(s, 2)
        total = yown[h, u]
        for i in range(2):
            arrived(y2r.at[i, h, u], sem("y2", i, h, u))
            total = total + y2r[i, h, u].astype(F32)
        yown[h, u] = total
        zs[h, u] = total.astype(BF16)
        for k in (2, 1, 3):
            to = plus(zl, k)
            send(zs.at[h, u, to], zr.at[h, u, k - 1], dev(zl_=to), sem("z", k, s))

    def ca(_):
        ct_load.wait()
        for i, device in enumerate((y_up, y_down)):
            part = ct_v.at[y, pl.ds(i * 256, 256)]
            send(part, part, device, sem("ca", i))

    def cb(_):
        for i, device in enumerate((y_up, y_down)):
            part = ct_v.at[y, pl.ds(256 - i * 256, 256)]
            send(part, part, device, sem("cb", i))

    def cf(_):
        for i, device in enumerate((y_up, y_down)):
            part = ct_v.at[plus(y, 3 - 2 * i), pl.ds(i * 256, 256)]
            arrived(part, sem("ca", i))
            send(part, part, device, sem("cf", i))

    def z2(s):
        h, u = divmod(s, 2)
        total = yown[h, u, zl]
        for k in (1, 2, 3):
            arrived(zr.at[h, u, k - 1], sem("z", k, s))
            total = total + zr[h, u, k - 1].astype(F32)
        proj[h, u, zl] = total.astype(BF16)
        for k in (2, 1, 3):
            send(proj.at[h, u, zl], proj.at[h, u, zl], dev(zl_=plus(zl, k)), sem("za", k, s))

    def dt(s):
        h, u = divmod(s, 2)
        if s == 0:
            for i in range(2):
                arrived(ct_v.at[plus(y, 3 - 2 * i), pl.ds(256 - i * 256, 256)], sem("cb", i))
                arrived(ct_v.at[plus(y, 2), pl.ds(i * 256, 256)], sem("cf", i))
        for k in (1, 2, 3):
            arrived(proj.at[h, u, plus(zl, 4 - k)], sem("za", k, s))
        left = proj[h, u].reshape(256, 128)
        for b in range(4):
            right = jnp.concatenate([ct_v[b, (2 * z + u) * 64 : (2 * z + u) * 64 + 64] for z in range(4)], axis=0)
            block = lax.dot_general(left, right, (((0,), (0,)), ((), ())), preferred_element_type=F32)
            block = block.reshape(2, 2, 32, 256)
            for i in range(2):
                for cc in range(2):
                    if u == 0:
                        plow[h, cc, i, b] = block[i, cc]
                    else:
                        plow[h, cc, i, b] += block[i, cc]
        if u == 1:
            cs[h] = plow[h, other].astype(BF16)
            send(cs.at[h], cr.at[h], dev(c_=other), sem("c", h))

    def bx(h):
        arrived(cr.at[h], sem("c", h))
        total = plow[h, c] + cr[h].astype(F32)
        csum[h] = total
        xs[h] = total.astype(BF16)
        for k in (2, 1, 3):
            to = plus(x, k)

            @pl.when(lax.div(to, 2) == h)
            def _():
                send(
                    xs.at[h, lax.rem(to, 2)], xr.at[k - 1], dev(x_=to), sem("x", k),
                    like=lambda: xs.at[0, 0], cond=lambda k=k: lax.div(plus(x, k), 2) == h,
                )

    def bh(h):
        @pl.when(xh == h)
        def _():
            total = csum[h, xx]
            for k in (1, 3, 2):
                arrived(xr.at[k - 1], sem("x", k))
                total = total + xr[k - 1].astype(F32)
            xsum[...] = total
            hs[...] = total.astype(BF16)
            for k in (2, 1, 3):
                to = plus(zh, k)
                send(
                    hs.at[to], hr.at[k - 1], dev(zh_=to), sem("h", k),
                    like=lambda: hs.at[0], cond=lambda: xh == h,
                )

    def moments(m, low):
        return 0.9 * m[0] + 0.1 * low, 0.999 * m[1] + 0.001 * low * low

    def ad(h):
        @pl.when(moved & (xh == h))
        def _():
            arrived(mr_v, sem("m"))

        @pl.when(xh == h)
        def _():
            total = xsum[zh]
            for k in (1, 3, 2):
                arrived(hr.at[k - 1], sem("h", k))
                total = total + hr[k - 1].astype(F32)
            low = total / REPLICAS
            low_v[...] = low
            first, second = moments(mr_v, low)
            first_hat = first / (1.0 - 0.9**STEP)
            second_hat = second / (1.0 - 0.999**STEP)
            update = (first_hat / (jnp.sqrt(second_hat) + 1e-08)).astype(BF16)
            upd[0] = update[:, :128]
            upd[1] = update[:, 128:]
            place = need.at[y, x, c]
            at = sem("n", 0, 0, 0) + x * 2 + c
            for k in (2, 1, 3, 0):
                for same in (0, 1):
                    half = c if same else other
                    device = dev(x_=zl, c_=half, zl_=plus(zl, k))
                    index = sem("n", 1, k, same)
                    rest = dict(like=lambda: upd.at[0])
                    if k == 0 and same:

                        @pl.when(apart)
                        def _():
                            send(upd.at[c], place, device, index, at, cond=lambda: apart & (xh == h), **rest)

                        @pl.when(jnp.logical_not(apart))
                        def _():
                            need[y, x, c] = upd[c]
                    else:
                        send(upd.at[half], place, device, index, at, cond=lambda: xh == h, **rest)

        @pl.when((xh == h) & moved)
        def _():
            send(low_v, back, swapped, sem("b"), like=lambda: back, cond=lambda: (xh == h) & moved)

    def c1(h):
        for i in (2 * h, 2 * h + 1):
            for cc in range(2):

                @pl.when(jnp.logical_or(apart, jnp.logical_or(i != x, cc != c)))
                def _():
                    arrived(need.at[y, i, cc], sem("n", 0, i, cc))

        mine = need.at[y, pl.ds(2 * h, 2)]
        for k in (2, 1, 3):
            send(mine, mine, dev(y_=plus(y, k)), sem("g", k, h))

    def d(h):
        for k in (1, 3, 2):
            arrived(need.at[plus(y, 4 - k), pl.ds(2 * h, 2)], sem("g", k, h))
        if h == 1:
            w_load.wait()
        lower = [need[a, 2 * h : 2 * h + 2].reshape(128, 128) for a in range(4)]
        for r in range(0, 1024, 256):
            span = slice(r, r + 256)
            change = sum(dot(p_v[a, span, h * 128 : h * 128 + 128], lower[a]) for a in range(4))
            if h == 0:
                acc[span] = change
            else:
                nw_v[span] = (w_v[span].astype(F32) - 0.5 * (acc[span] + change)).astype(BF16)
                leaving.append(load(nw_v.at[pl.ds(r, 256)], ow.at[pl.ds(r, 256)]))

    def own(_):
        @pl.when(moved)
        def _():
            arrived(back, sem("b"))

        @pl.when(jnp.logical_not(moved))
        def _():
            back[...] = low_v[...]

        nm_v[0], nm_v[1] = moments(m_v, back[...])
        leaving.append(load(nm_v.at[0], o1))
        leaving.append(load(nm_v.at[1], o2))

    for i in range(4):
        for cc in range(2):
            sem("n", 0, i, cc)
    plan = [(m0, 0)] + [(y1, s) for s in range(4)]
    plan += [(z1, 0), (ca, 0), (z1, 1), (cb, 0), (z1, 2), (z1, 3), (hop, 0), (cf, 0)]
    plan += [(z2, s) for s in range(4)] + [(dt, s) for s in range(4)] + [(mo, 0), (bx, 0), (bx, 1)]
    plan += [(stage, h) for stage in (bh, ad, c1, d) for h in range(2)]
    plan += [(own, 0)]

    for stage, index in plan:
        stage(index)

    for copy in leaving:
        copy.wait()
    for like, index, cond in waits:
        wait = copy_of(like(), like(), dev(c_=other), index).wait_send
        if cond is None:
            wait()
        else:
            pl.when(cond())(wait)


def leave(a, b, c, oa, ob, oc):
    oa[...] = a[...]
    ob[...] = b[...]
    oc[...] = c[...]


def local(weight, inputs, cotangent, projector, first_moment, second_moment):
    v = pltpu.VMEM
    shapes = (
        jax.ShapeDtypeStruct((1024, 128), BF16),
        jax.ShapeDtypeStruct((32, 256), F32),
        jax.ShapeDtypeStruct((32, 256), F32),
    )
    results = pl.pallas_call(
        kernel,
        out_shape=shapes,
        in_specs=[pl.BlockSpec(memory_space=pl.ANY)] * 6,
        out_specs=[pl.BlockSpec(memory_space=pl.ANY)] * 3,
        scratch_shapes=[
            v((1024, 128), BF16),
            v((512, 1024), BF16),
            v((4, 512, 256), BF16),
            v((4, 1024, 256), BF16),
            v((2, 32, 256), F32),
            v((2, 32, 256), F32),
            v((2, 2, 4, 64, 128), BF16),
            v((2, 2, 2, 2, 64, 128), BF16),
            v((2, 2, 2, 4, 64, 128), BF16),
            v((2, 2, 2, 4, 64, 128), BF16),
            v((2, 2, 2, 4, 64, 128), F32),
            v((2, 2, 4, 64, 128), F32),
            v((2, 2, 4, 64, 128), BF16),
            v((2, 2, 3, 64, 128), BF16),
            v((2, 2, 4, 64, 128), BF16),
            v((2, 2, 2, 4, 32, 256), F32),
            v((2, 2, 4, 32, 256), BF16),
            v((2, 2, 4, 32, 256), BF16),
            v((2, 2, 4, 32, 256), F32),
            v((2, 2, 4, 32, 256), BF16),
            v((3, 4, 32, 256), BF16),
            v((4, 32, 256), F32),
            v((4, 32, 256), BF16),
            v((3, 32, 256), BF16),
            v((32, 256), F32),
            v((32, 256), F32),
            v((2, 32, 128), BF16),
            v((4, 4, 2, 32, 128), BF16),
            v((1024, 128), F32),
            v((1024, 128), BF16),
            v((2, 32, 256), F32),
            pltpu.SemaphoreType.DMA((20,)),
            pltpu.SemaphoreType.DMA((96,)),
            pltpu.SemaphoreType.DMA((96,)),
            pltpu.SemaphoreType.REGULAR((2, 2)),
        ],
        compiler_params=pltpu.CompilerParams(
            collective_id=0, has_side_effects=True, vmem_limit_bytes=58 * 2**20
        ),
    )(weight, inputs, cotangent, projector, first_moment, second_moment)
    return pl.pallas_call(
        leave,
        out_shape=shapes,
        in_specs=[pl.BlockSpec(memory_space=pltpu.VMEM)] * 3,
        out_specs=[pl.BlockSpec(memory_space=pltpu.VMEM)] * 3,
        compiler_params=pltpu.CompilerParams(vmem_limit_bytes=58 * 2**20),
    )(*results)


def solution(mesh):
    placed = (
        P("tensor", "dp"),
        P("dp", "tensor"),
        P("dp", "tensor"),
        P("tensor", None),
        P("dp", "tensor"),
        P("dp", "tensor"),
    )
    return jax.shard_map(
        local,
        mesh=mesh,
        in_specs=placed,
        out_specs=(P("tensor", "dp"), P("dp", "tensor"), P("dp", "tensor")),
        check_vma=False,
    )
```
